32 devices in a mesh: gx: 4 (over y, core), gy: 8 (over z, x).
Axes of the slice: x: 2, y: 2, z: 4, core: 2. Of those that a mesh axis runs over, the one named last changes fastest.
Arguments:
- adjoint_in: float32 [19, 4, 64, 1024], P(None, None, 'gx', 'gy'), may hold values from -6 to 6
- forward_pops: bfloat16 [2, 19, 4, 64, 1024], P(None, None, None, 'gx', 'gy'), may hold values from 0 to 0.42, as said below
- solid_mask: int32 [4, 64, 1024], P(None, 'gx', 'gy'), may hold values 0 or 1
- region_label: int32 [64, 1024], P('gx', 'gy'), may hold values from 0 to 2
- design: float32 [64, 1024], P('gx', 'gy'), may hold values from 0 to 1
Outputs:
- adjoint_out: float32 [19, 4, 64, 1024], P(None, None, 'gx', 'gy')
- sensitivity: float32 [64, 1024], P('gx', 'gy')
The draws below stay inside these ranges and needn't reach their ends.
Inputs may be any that keep to these rules, and one draw needn't show every extreme that they name: `forward_pops`: each population lies between 0.75 and 1.25 times its lattice weight.
All inputs are finite; a program needn't handle non-finite values. No bound on the sum of `solid_mask` on one device may be relied on, other than what follows from the above.
Results may differ from the reference program's by a relative error of at most 0.0004.
Values sent between devices are 32-bit elements; how exact they have to be, the bound alone decides.
A program may use at most 128 MiB of HBM per device.

```python
import jax
import jax.numpy as jnp
from jax import lax

NZ = 4
SWEEPS = 4
NX = 64
NY = 1024


def draw_forward_pops(key, part):
    weights = jnp.asarray([1.0 / 3.0] + [1.0 / 18.0] * 6 + [1.0 / 36.0] * 12, jnp.float32).reshape(1, 19, 1, 1, 1)
    shape_all = (2, 19, NZ, NX, NY)
    factor = 1.0 + 0.1 * jnp.clip(jax.random.normal(key, shape_all, jnp.float32), -2.5, 2.5)
    return (weights * factor).astype(jnp.bfloat16)


def touch_ends(values, key, low, high):
    spot = [jax.random.randint(jax.random.fold_in(key, axis), (), 0, length) for axis, length in enumerate(values.shape)]
    widest = values.shape.index(max(values.shape))
    neighbour = spot[:widest] + [(spot[widest] + 1) % values.shape[widest]] + spot[widest + 1:]
    return values.at[tuple(spot)].set(low).at[tuple(neighbour)].set(high)


def block_levels(own_key, dims, cuts, smallest, top_value):
    gain, own = 1.0, jax.random.fold_in(own_key, 6)
    for position, shards_of in cuts:
        draws = jnp.exp(jax.random.uniform(jax.random.fold_in(own, position), (shards_of,), jnp.float32, smallest / len(cuts), top_value / len(cuts)))
        gain = gain * jnp.repeat(draws, dims[position] // shards_of).reshape([-1 if axis == position else 1 for axis in range(len(dims))])
    return gain


def bell_draw(own_key, extent, width, bound, shards=(), held_as=jnp.bfloat16):
    array = width * jax.random.normal(own_key, extent, jnp.float32)
    if shards:
        array = array * block_levels(own_key, extent, shards, -0.22, 0.18)
    return jnp.clip(array, -bound, bound).astype(held_as)


def setup_inputs(seed: int = 0) -> dict:
    key_list = jax.random.split(jax.random.key(seed), 6)
    return {
        "adjoint_in": bell_draw(key_list[0], (19, NZ, NX, NY), 1.0, 6.0, ((2, 4), (3, 8)), jnp.float32),
        "forward_pops": draw_forward_pops(jax.random.fold_in(key_list[5], 71), 0),
        "solid_mask": touch_ends((jax.random.randint(key_list[2], (NZ, NX, NY), 0, 6) < 1).astype(jnp.int32), jax.random.fold_in(key_list[2], 1), 0, 1),
        "region_label": touch_ends(jax.random.randint(key_list[3], (NX, NY), 0, 3), jax.random.fold_in(key_list[3], 1), 0, 2).astype(jnp.int32),
        "design": jnp.clip(1.0 * jax.random.uniform(key_list[4], (NX, NY), jnp.float32) ** block_levels(key_list[4], (NX, NY), ((0, 4), (1, 8)), -0.2, 0.2), 0.0, 1.0),
    }


VELOCITIES = [(0, 0, 0), (1, 0, 0), (-1, 0, 0), (0, 1, 0), (0, -1, 0), (0, 0, 1), (0, 0, -1), (1, 1, 0), (-1, -1, 0), (1, -1, 0), (-1, 1, 0), (1, 0, 1), (-1, 0, -1), (1, 0, -1), (-1, 0, 1), (0, 1, 1), (0, -1, -1), (0, 1, -1), (0, -1, 1)]
OPPOSITE = [0, 2, 1, 4, 3, 6, 5, 8, 7, 10, 9, 12, 11, 14, 13, 16, 15, 18, 17]
WEIGHTS = [1.0 / 3.0] + [1.0 / 18.0] * 6 + [1.0 / 36.0] * 12
RELAX_RATES = [0.0] * 4 + [1.6] * 6 + [1.4] * 6 + [1.2] * 3
EXPONENTS = [(0, 0, 0), (1, 0, 0), (0, 1, 0), (0, 0, 1), (2, 0, 0), (0, 2, 0), (0, 0, 2), (1, 1, 0), (1, 0, 1), (0, 1, 1), (2, 1, 0), (2, 0, 1), (1, 2, 0), (0, 2, 1), (1, 0, 2), (0, 1, 2), (2, 2, 0), (2, 0, 2), (0, 2, 2)]
BLOCK_LIMIT = 0.5
SENSE_SCALE = 20.0
FILTER_WEIGHT = 16.0

def moment_table():
    rows_out = []
    for expo in EXPONENTS:
        vector = [float(vel[0] ** expo[0] * vel[1] ** expo[1] * vel[2] ** expo[2]) for vel in VELOCITIES]
        for prior in rows_out:
            factor = sum((a * b for a, b in zip(vector, prior))) / sum((b * b for b in prior))
            vector = [a - factor * b for a, b in zip(vector, prior)]
        rows_out.append(vector)
    norms = [sum((b * b for b in row)) for row in rows_out]
    table = []
    for first in range(19):
        line = []
        for second in range(19):
            line.append(sum((rows_out[k][first] / norms[k] * RELAX_RATES[k] * rows_out[k][second] for k in range(19))))
        table.append(line)
    return table

def collide(popul, blocking):
    relax_matrix = jnp.asarray(moment_table(), jnp.float32)
    veloc = jnp.asarray(VELOCITIES, jnp.float32)
    weights = jnp.asarray(WEIGHTS, jnp.float32)
    density = lax.optimization_barrier(jnp.sum(popul, axis=0))
    momentum = jnp.dot(veloc.T, popul, precision=lax.Precision.HIGHEST)
    velocity = momentum / density
    along_u = jnp.dot(veloc, velocity, precision=lax.Precision.HIGHEST)
    speed_sq = lax.optimization_barrier(jnp.sum(velocity * velocity, axis=0))
    equilib = weights[:, None] * density * (1.0 + 3.0 * along_u + 4.5 * along_u * along_u - 1.5 * speed_sq)
    relaxed = popul - jnp.dot(relax_matrix, popul - equilib, precision=lax.Precision.HIGHEST)
    reflected = popul[jnp.asarray(OPPOSITE, jnp.int32)]
    return ((1.0 - blocking) * relaxed + blocking * reflected, reflected - relaxed)

def adjoint_cell(saved_now, pulled, blocking, lever):

    def forward(popul):
        return collide(popul, blocking)
    _, back_fn, change = jax.vjp(forward, saved_now, has_aux=True)
    result, = back_fn(pulled)
    term = lax.optimization_barrier(jnp.sum(pulled * change, axis=0)) * lever
    return (result, term)

def pull_back(padded, width_x, width_y):
    pieces = []
    for slot in range(19):
        step_x, step_y, step_z = VELOCITIES[slot]
        piece = padded[slot, :, 1 + step_x:1 + step_x + width_x, 1 + step_y:1 + step_y + width_y]
        pieces.append(jnp.roll(piece, -step_z, axis=0))
    return jnp.stack(pieces)

def reference(adjoint_in, forward_pops, solid_mask, region_label, design):
    width_x, width_y = design.shape
    inside = region_label > 0
    blocking = jnp.where(solid_mask == 1, 1.0, jnp.where(inside[None], BLOCK_LIMIT * design[None], 0.0)).astype(jnp.float32)
    lever = jnp.where((solid_mask == 0) & inside[None], BLOCK_LIMIT, 0.0).astype(jnp.float32)
    adjoint = adjoint_in
    raw = jnp.zeros((width_x, width_y), jnp.float32)
    for section in (1, 0):
        padded = jnp.pad(adjoint, ((0, 0), (0, 0), (1, 1), (1, 1)))
        pulled = pull_back(padded, width_x, width_y)
        saved_now = forward_pops[section].astype(jnp.float32)

        def per_plane(items):
            saved_plane, pulled_plane, block_plane, lever_plane = items
            result, term = adjoint_cell(saved_plane.reshape(19, -1), pulled_plane.reshape(19, -1), block_plane.reshape(-1), lever_plane.reshape(-1))
            return (result.reshape(19, width_x, width_y), term.reshape(width_x, width_y))
        results, terms = lax.map(per_plane, (jnp.moveaxis(saved_now, 1, 0), jnp.moveaxis(pulled, 1, 0), blocking, lever))
        adjoint = jnp.moveaxis(results, 0, 1)
        raw = raw + lax.optimization_barrier(jnp.sum(terms, axis=0))
    raw = SENSE_SCALE * raw
    smooth = raw
    for sweep in range(SWEEPS):
        framed = jnp.pad(smooth, 1)
        beside_all = framed[:-2, 1:-1] + framed[2:, 1:-1] + framed[1:-1, :-2] + framed[1:-1, 2:]
        smooth = (raw + FILTER_WEIGHT * beside_all) / (1.0 + 4.0 * FILTER_WEIGHT)
    region_one = (region_label == 1).astype(jnp.float32)
    region_two = (region_label == 2).astype(jnp.float32)
    mean_one = jnp.sum(smooth * region_one) / jnp.maximum(jnp.sum(region_one), 1.0)
    mean_two = jnp.sum(smooth * region_two) / jnp.maximum(jnp.sum(region_two), 1.0)
    sensitivity = region_one * (smooth - mean_one) + region_two * (smooth - mean_two)
    return (adjoint, sensitivity)
```

```python
import functools

import jax
import jax.numpy as jnp
from jax import lax
from jax.experimental import pallas as pl
from jax.experimental.pallas import tpu as pltpu
from jax.sharding import PartitionSpec as P

SWEEPS = 4
VELOCITIES = [
    (0, 0, 0),
    (1, 0, 0),
    (-1, 0, 0),
    (0, 1, 0),
    (0, -1, 0),
    (0, 0, 1),
    (0, 0, -1),
    (1, 1, 0),
    (-1, -1, 0),
    (1, -1, 0),
    (-1, 1, 0),
    (1, 0, 1),
    (-1, 0, -1),
    (1, 0, -1),
    (-1, 0, 1),
    (0, 1, 1),
    (0, -1, -1),
    (0, 1, -1),
    (0, -1, 1),
]
PAIRS = [VELOCITIES[2 * k + 1] for k in range(9)]
BLOCK_LIMIT = 0.5
SENSE_SCALE = 20.0
FILTER_WEIGHT = 16.0
MESH = pl.DeviceIdType.MESH
F32 = jnp.float32

DIRS = [(-1, 0), (1, 0), (0, -1), (0, 1), (-1, -1), (-1, 1), (1, -1), (1, 1)]


def pops_with(cx=None, cy=None):
    return [
        i
        for i, v in enumerate(VELOCITIES)
        if (cx is None or v[0] == cx) and (cy is None or v[1] == cy)
    ]


def add_all(terms):
    terms = list(terms)
    while len(terms) > 1:
        terms = [
            terms[k] + terms[k + 1] if k + 1 < len(terms) else terms[k]
            for k in range(0, len(terms), 2)
        ]
    return terms[0]


def along(values, axis):
    total = None
    for vel, val in zip(PAIRS, values):
        if vel[axis] == 0:
            continue
        if total is None:
            total = val if vel[axis] > 0 else -val
        else:
            total = total + val if vel[axis] > 0 else total - val
    return total


def dotted(vec, vel):
    total = None
    for comp, c in zip(vec, vel):
        if c == 0:
            continue
        if total is None:
            total = comp if c > 0 else -comp
        else:
            total = total + comp if c > 0 else total - comp
    return total


def adjoint_cell(f, a, blocking):
    fe = [f[2 * k + 1] + f[2 * k + 2] for k in range(9)]
    fo = [f[2 * k + 1] - f[2 * k + 2] for k in range(9)]
    rho = add_all([f[0]] + fe)
    inv = 1.0 / rho
    u = [along(fo, d) * inv for d in range(3)]
    usq = u[0] * u[0] + u[1] * u[1] + u[2] * u[2]

    e = [a[2 * k + 1] + a[2 * k + 2] for k in range(9)]
    o = [a[2 * k + 1] - a[2 * k + 2] for k in range(9)]
    mom = [0.28 * along(o, d) for d in range(3)]
    big_o = [1.4 * o[k] - dotted(mom, PAIRS[k]) for k in range(9)]
    edge = [e[3] + e[4], e[5] + e[6], e[7] + e[8]]
    axis_sum = e[0] + e[1] + e[2]
    edge_sum = edge[0] + edge[1] + edge[2]
    mean16 = (1.6 / 19.0) * (a[0] + axis_sum + edge_sum)
    a4 = 4.0 * a[0]
    t = [
        edge[0] - 2.0 * (e[0] + e[1]) + a4,
        edge[1] - 2.0 * (e[0] + e[2]) + a4,
        edge[2] - 2.0 * (e[1] + e[2]) + a4,
    ]
    tsum = (2.0 / 7.0) * (t[0] + t[1] + t[2])
    p = [(0.4 / 12.0) * (tk - tsum) for tk in t]
    b0 = 1.6 * a[0] - mean16 - 4.0 * (p[0] + p[1] + p[2])
    q = [-2.0 * (p[0] + p[1]), -2.0 * (p[0] + p[2]), -2.0 * (p[1] + p[2])]
    shift = [2.0 * (mean16 + val) for val in q + p]
    plane = [0, 1, 2, 3, 3, 4, 4, 5, 5]
    big_e = [1.6 * e[k] - shift[plane[k]] for k in range(9)]

    c36 = 1.0 / 36.0
    s3, s5, s7 = big_e[3] + big_e[4], big_e[5] + big_e[6], big_e[7] + big_e[8]
    zeroth = (1.0 / 3.0) * b0 + c36 * (
        2.0 * (big_e[0] + big_e[1] + big_e[2]) + s3 + s5 + s7
    )
    xx = c36 * (2.0 * big_e[0] + s3 + s5)
    yy = c36 * (2.0 * big_e[1] + s3 + s7)
    zz = c36 * (2.0 * big_e[2] + s5 + s7)
    xy = c36 * (big_e[3] - big_e[4])
    xz = c36 * (big_e[5] - big_e[6])
    yz = c36 * (big_e[7] - big_e[8])
    weighted = [2.0 * big_o[k] if k < 3 else big_o[k] for k in range(9)]
    first = [c36 * along(weighted, d) for d in range(3)]
    bu = [
        xx * u[0] + xy * u[1] + xz * u[2],
        xy * u[0] + yy * u[1] + yz * u[2],
        xz * u[0] + yz * u[1] + zz * u[2],
    ]
    ubu = 4.5 * (u[0] * bu[0] + u[1] * bu[1] + u[2] * bu[2])
    half_u = 1.5 * usq * zeroth
    scalar = zeroth + half_u - ubu
    vec = [3.0 * (first[d] - zeroth * u[d]) + 9.0 * bu[d] for d in range(3)]
    eq_b = zeroth - half_u + ubu + 3.0 * (
        first[0] * u[0] + first[1] * u[1] + first[2] * u[2]
    )

    open_part = 1.0 - blocking
    odd_keep = 1.0 - 2.0 * blocking
    result = [None] * 19
    result[0] = a[0] + open_part * (scalar - b0)
    half_open = 0.5 * open_part
    half_keep = 0.5 * odd_keep
    scalar2 = 2.0 * scalar
    vec2 = [2.0 * val for val in vec]
    for k in range(9):
        even = 0.5 * e[k] + half_open * (scalar2 - big_e[k])
        odd = half_keep * o[k] + half_open * (dotted(vec2, PAIRS[k]) - big_o[k])
        result[2 * k + 1] = even + odd
        result[2 * k + 2] = even - odd
    parts = [b0 * f[0] - rho * eq_b]
    for k in range(9):
        parts.append(0.5 * (big_e[k] * fe[k] + big_o[k] * fo[k]) - fo[k] * o[k])
    return result, add_all(parts)


def kernel(
    nx,
    ny,
    adj_hbm,
    pops_hbm,
    solid_hbm,
    label_hbm,
    design_hbm,
    out_ref,
    sens_ref,
    adj,
    pops,
    solid,
    label,
    design,
    mid,
    pull,
    send1,
    recv1,
    send2,
    recv2,
    send3,
    recv3,
    gath1,
    gath2,
    part1,
    part2,
    in_sem,
    s_sem,
    r_sem,
    g1s_sem,
    g1r_sem,
    g2s_sem,
    g2r_sem,
):
    mx, my = lax.axis_index("gx"), lax.axis_index("gy")

    def has(d):
        conds = []
        if d[0] < 0:
            conds.append(mx > 0)
        if d[0] > 0:
            conds.append(mx < nx - 1)
        if d[1] < 0:
            conds.append(my > 0)
        if d[1] > 0:
            conds.append(my < ny - 1)
        return functools.reduce(jnp.logical_and, conds)

    barrier = pltpu.get_barrier_semaphore()
    for k in range(1, nx):
        pl.semaphore_signal(
            barrier, inc=1, device_id=(lax.rem(mx + k, nx), my), device_id_type=MESH
        )
    for k in range(1, ny):
        pl.semaphore_signal(
            barrier, inc=1, device_id=(mx, lax.rem(my + k, ny)), device_id_type=MESH
        )
    for d in DIRS[4:]:

        @pl.when(has(d))
        def _():
            pl.semaphore_signal(
                barrier, inc=1, device_id=(mx + d[0], my + d[1]), device_id_type=MESH
            )

    loads = [
        pltpu.make_async_copy(src, dst, in_sem.at[k])
        for k, (src, dst) in enumerate(
            [
                (adj_hbm, adj),
                (label_hbm, label),
                (pops_hbm, pops),
                (solid_hbm, solid),
                (design_hbm, design),
            ]
        )
    ]
    for load in loads:
        load.start()

    for n, d in enumerate(DIRS):

        @pl.when(jnp.logical_not(has((-d[0], -d[1]))))
        def _():
            for buf in (recv1, recv2, recv3):
                buf[n] = jnp.zeros(buf.shape[1:], F32)

    lane = lax.broadcasted_iota(jnp.int32, (16, 128), 1)
    lane4 = lax.broadcasted_iota(jnp.int32, (4, 128), 1)

    def copies(rnd, send, recv):
        out = []
        for n, d in enumerate(DIRS):
            rows = {0: (32, 16, 16), 1: (24, 16, 8), 2: (8, 16, 8)}[rnd][
                0 if d[1] == 0 else (1 if d[0] == 0 else 2)
            ]
            start = 0
            if rnd == 2 and d[0] > 0:
                start = 8
            src = send.at[pl.ds(start, rows)] if rnd == 2 else send.at[n, pl.ds(0, rows)]
            out.append(
                pltpu.make_async_remote_copy(
                    src_ref=src,
                    dst_ref=recv.at[n, pl.ds(0, rows)],
                    send_sem=s_sem.at[rnd, n],
                    recv_sem=r_sem.at[rnd, n],
                    device_id=(mx + d[0], my + d[1]),
                    device_id_type=MESH,
                )
            )
        return out

    def start_all(cps):
        for n, d in enumerate(DIRS):

            @pl.when(has(d))
            def _():
                cps[n].start()

    def recv_all(cps):
        for n, d in enumerate(DIRS):

            @pl.when(has((-d[0], -d[1])))
            def _():
                cps[n].wait_recv()

    def send_done(cps):
        for n, d in enumerate(DIRS):

            @pl.when(has(d))
            def _():
                cps[n].wait_send()

    def pack(src, send, region):
        for n, (dx, dy) in enumerate(DIRS):
            if dy == 0:
                row = 0 if dx < 0 else 15
                for j, i in enumerate(pops_with(cx=-dx)):
                    for z in range(4):
                        send[n, 4 * j + z : 4 * j + z + 1] = src[i, z, row : row + 1, :]
                if region is not None:
                    send[n, 24:32] = region[0:8] if dx < 0 else region[8:16]
            elif dx == 0:
                at = 0 if dy < 0 else 127
                base = 64 if dy < 0 else 0
                acc = region if region is not None else jnp.zeros((16, 128), F32)
                for j, i in enumerate(pops_with(cy=-dy)):
                    for z in range(4):
                        to = base + 4 * j + z
                        moved = pltpu.roll(src[i, z], (to - at) % 128, 1)
                        acc = jnp.where(lane == to, moved, acc)
                send[n, 0:16] = acc
            else:
                row = 0 if dx < 0 else 15
                i = VELOCITIES.index((-dx, -dy, 0))
                for z in range(4):
                    send[n, z : z + 1] = src[i, z, row : row + 1, :]
                if region is not None:
                    send[n, 8:16] = region[0:8] if dx < 0 else region[8:16]

    def pull_local(src):
        for i, (cx, cy, cz) in enumerate(VELOCITIES):
            for z in range(4):
                val = src[i, z]
                if cy != 0:
                    val = pltpu.roll(val, (-cy) % 128, 1)
                pull[i, z, 8:24] = val

    def pull_edges(recv):
        for n, (dx, dy) in enumerate(DIRS):
            if dx == 0:
                base = 64 if dy < 0 else 0
                at = 127 if dy < 0 else 0
                got = recv[n, 0:16]
                for j, i in enumerate(pops_with(cy=-dy)):
                    for z in range(4):
                        moved = pltpu.roll(got, (at - base - 4 * j - z) % 128, 1)
                        pull[i, z, 8:24] = jnp.where(lane == at, moved, pull[i, z, 8:24])
            elif dy == 0:
                row = 24 if dx < 0 else 7
                for j, i in enumerate(pops_with(cx=-dx)):
                    cy = VELOCITIES[i][1]
                    val = recv[n, 4 * j : 4 * j + 4]
                    if cy != 0:
                        val = pltpu.roll(val, (-cy) % 128, 1)
                        corner = recv[DIRS.index((dx, -cy)), 0:4]
                        corner = pltpu.roll(corner, (-cy) % 128, 1)
                        val = jnp.where(lane4 == (127 if cy > 0 else 0), corner, val)
                    for z in range(4):
                        pull[i, z, row : row + 1] = val[z : z + 1]

    def cells(section, dst):
        total = None
        for z in range(4):
            f = [pops[section, i, z].astype(F32) for i in range(19)]
            a = []
            for i, (cx, cy, cz) in enumerate(VELOCITIES):
                a.append(pull[i, (z + cz) % 4, 8 + cx : 24 + cx, :])
            is_solid = solid[z] == 1
            inside = label[...] > 0
            blocking = jnp.where(
                is_solid, 1.0, jnp.where(inside, BLOCK_LIMIT * design[...], 0.0)
            )
            lever = jnp.where(
                jnp.logical_and(jnp.logical_not(is_solid), inside), BLOCK_LIMIT, 0.0
            )
            result, term = adjoint_cell(f, a, blocking)
            for i in range(19):
                dst[i, z] = result[i]
            term = term * lever
            total = term if total is None else total + term
        return total

    wide_row = lax.broadcasted_iota(jnp.int32, (32, 256), 0)
    wide_lane = lax.broadcasted_iota(jnp.int32, (32, 256), 1)
    gone = jnp.logical_or(
        jnp.logical_or(
            jnp.logical_and(wide_row >= 24, mx == 0),
            jnp.logical_and(
                jnp.logical_and(wide_row >= 16, wide_row < 24), mx == nx - 1
            ),
        ),
        jnp.logical_or(
            jnp.logical_and(wide_lane >= 192, my == 0),
            jnp.logical_and(
                jnp.logical_and(wide_lane >= 128, wide_lane < 192), my == ny - 1
            ),
        ),
    )
    scale_den = 1.0 / (1.0 + 4.0 * FILTER_WEIGHT)
    keep = jnp.where(gone, 0.0, scale_den)

    def widened(own, get):
        low = lane[0:8] < 64
        top = jnp.concatenate(
            [own, jnp.where(lane < 64, get((0, -1)), get((0, 1)))], axis=1
        )
        down = jnp.concatenate(
            [get((-1, 0)), jnp.where(low, get((-1, -1)), get((-1, 1)))], axis=1
        )
        up = jnp.concatenate(
            [get((1, 0)), jnp.where(low, get((1, -1)), get((1, 1)))], axis=1
        )
        return jnp.concatenate([top, down, up], axis=0)

    def jacobi(start):
        base = start * keep
        weight = FILTER_WEIGHT * keep
        smooth = jnp.where(gone, 0.0, start)
        for _ in range(SWEEPS):
            beside = (
                pltpu.roll(smooth, 1, 0)
                + pltpu.roll(smooth, 31, 0)
                + pltpu.roll(smooth, 1, 1)
                + pltpu.roll(smooth, 255, 1)
            )
            smooth = base + weight * beside
        return smooth

    loads[0].wait()
    loads[1].wait()
    region = label[...].astype(F32)
    pack(adj, send1, region)
    met = (nx - 1) + (ny - 1)
    for d in DIRS[4:]:
        met = met + has(d).astype(jnp.int32)
    pl.semaphore_wait(barrier, met)
    cps1 = copies(0, send1, recv1)
    start_all(cps1)
    pull_local(adj)
    for load in loads[2:]:
        load.wait()
    recv_all(cps1)
    pull_edges(recv1)
    raw1 = cells(1, mid)

    pack(mid, send2, None)
    cps2 = copies(1, send2, recv2)
    start_all(cps2)
    pull_local(mid)

    def label_of(d):
        n = DIRS.index(d)
        if d[1] == 0:
            return recv1[n, 24:32]
        if d[0] == 0:
            return recv1[n, 0:16]
        return recv1[n, 8:16]

    wide_label = widened(region, label_of)
    share = []
    for r in (1.0, 2.0):
        share.append(jacobi(jnp.where(wide_label == r, 1.0, 0.0))[0:16, 0:128])

    def folded(one, two):
        one = jnp.sum(one, axis=0, keepdims=True)
        two = jnp.sum(two, axis=0, keepdims=True)
        one = one + pltpu.roll(one, 64, 1)
        two = two + pltpu.roll(two, 64, 1)
        return jnp.where(lane[0:1] < 64, one, two)

    part1[...] = jnp.zeros((8, 128), F32)
    part1[1:2] = folded(jnp.where(region == 1.0, 1.0, 0.0), jnp.where(region == 2.0, 1.0, 0.0))

    recv_all(cps2)
    pull_edges(recv2)
    raw2 = cells(0, out_ref)
    raw = SENSE_SCALE * (raw1 + raw2)
    send3[...] = raw
    part1[0:1] = folded(raw * share[0], raw * share[1])

    def gather(part, slots, send_sem, recv_sem, count, along_x):
        out = []
        for k in range(1, count):
            if along_x:
                peer = (lax.rem(mx + k, count), my)
            else:
                peer = (mx, lax.rem(my + k, count))
            out.append(
                pltpu.make_async_remote_copy(
                    src_ref=part,
                    dst_ref=slots.at[k - 1],
                    send_sem=send_sem.at[k - 1],
                    recv_sem=recv_sem.at[k - 1],
                    device_id=peer,
                    device_id_type=MESH,
                )
            )
        return out

    g1 = gather(part1, gath1, g1s_sem, g1r_sem, nx, True)
    for cp in g1:
        cp.start()
    cps3 = copies(2, send3, recv3)
    start_all(cps3)
    total = part1[...]
    for k, cp in enumerate(g1):
        cp.wait_recv()
        total = total + gath1[k]
    part2[...] = total
    g2 = gather(part2, gath2, g2s_sem, g2r_sem, ny, False)
    for cp in g2:
        cp.start()

    recv_all(cps3)

    def raw_of(d):
        n = DIRS.index(d)
        return recv3[n, 0:16] if d[0] == 0 else recv3[n, 0:8]

    smooth = jacobi(widened(raw, raw_of))[0:16, 0:128]
    for k, cp in enumerate(g2):
        cp.wait_recv()
        total = total + gath2[k]
    lane8 = lane[0:8] < 64
    ones = jnp.sum(jnp.where(lane8, total, 0.0), axis=1, keepdims=True)
    twos = jnp.sum(jnp.where(lane8, 0.0, total), axis=1, keepdims=True)
    mean1 = ones[0:1] / jnp.maximum(ones[1:2], 1.0)
    mean2 = twos[0:1] / jnp.maximum(twos[1:2], 1.0)
    sens_ref[...] = jnp.where(
        region == 1.0, smooth - mean1, jnp.where(region == 2.0, smooth - mean2, 0.0)
    )
    send_done(cps1)
    send_done(cps2)
    send_done(cps3)
    for cp in g1 + g2:
        cp.wait_send()


def per_device(nx, ny, adjoint_in, forward_pops, solid_mask, region_label, design):
    vmem, dma = pltpu.VMEM, pltpu.SemaphoreType.DMA
    return pl.pallas_call(
        functools.partial(kernel, nx, ny),
        out_shape=(
            jax.ShapeDtypeStruct(adjoint_in.shape, F32),
            jax.ShapeDtypeStruct(design.shape, F32),
        ),
        in_specs=[pl.BlockSpec(memory_space=pl.ANY)] * 5,
        out_specs=(
            pl.BlockSpec(memory_space=pltpu.VMEM),
            pl.BlockSpec(memory_space=pltpu.VMEM),
        ),
        scratch_shapes=[
            vmem(adjoint_in.shape, F32),
            vmem(forward_pops.shape, jnp.bfloat16),
            vmem(solid_mask.shape, jnp.int32),
            vmem(region_label.shape, jnp.int32),
            vmem(design.shape, F32),
            vmem(adjoint_in.shape, F32),
            vmem((19, 4, 32, 128), F32),
            vmem((8, 32, 128), F32),
            vmem((8, 32, 128), F32),
            vmem((8, 24, 128), F32),
            vmem((8, 24, 128), F32),
            vmem((16, 128), F32),
            vmem((8, 16, 128), F32),
            vmem((nx - 1, 8, 128), F32),
            vmem((ny - 1, 8, 128), F32),
            vmem((8, 128), F32),
            vmem((8, 128), F32),
            dma((5,)),
            dma((3, 8)),
            dma((3, 8)),
            dma((nx - 1,)),
            dma((nx - 1,)),
            dma((ny - 1,)),
            dma((ny - 1,)),
        ],
        compiler_params=pltpu.CompilerParams(
            collective_id=0, has_side_effects=True, vmem_limit_bytes=40 * 1024 * 1024
        ),
    )(adjoint_in, forward_pops, solid_mask, region_label, design)


def solution(mesh):
    in_specs = (
        P(None, None, "gx", "gy"),
        P(None, None, None, "gx", "gy"),
        P(None, "gx", "gy"),
        P("gx", "gy"),
        P("gx", "gy"),
    )
    out_specs = (P(None, None, "gx", "gy"), P("gx", "gy"))
    return jax.shard_map(
        functools.partial(per_device, mesh.shape["gx"], mesh.shape["gy"]),
        mesh=mesh,
        in_specs=in_specs,
        out_specs=out_specs,
        check_vma=False,
    )
```

```python
import functools

import jax
import jax.numpy as jnp
from jax import lax
from jax.experimental import pallas as pl
from jax.experimental.pallas import tpu as pltpu
from jax.sharding import PartitionSpec as P

SWEEPS = 4
VELOCITIES = [
    (0, 0, 0),
    (1, 0, 0),
    (-1, 0, 0),
    (0, 1, 0),
    (0, -1, 0),
    (0, 0, 1),
    (0, 0, -1),
    (1, 1, 0),
    (-1, -1, 0),
    (1, -1, 0),
    (-1, 1, 0),
    (1, 0, 1),
    (-1, 0, -1),
    (1, 0, -1),
    (-1, 0, 1),
    (0, 1, 1),
    (0, -1, -1),
    (0, 1, -1),
    (0, -1, 1),
]
PAIRS = [VELOCITIES[2 * k + 1] for k in range(9)]
BLOCK_LIMIT = 0.5
SENSE_SCALE = 20.0
FILTER_WEIGHT = 16.0
MESH = pl.DeviceIdType.MESH
F32 = jnp.float32

DIRS = [(-1, 0), (1, 0), (0, -1), (0, 1), (-1, -1), (-1, 1), (1, -1), (1, 1)]


def pops_with(cx=None, cy=None):
    return [
        i
        for i, v in enumerate(VELOCITIES)
        if (cx is None or v[0] == cx) and (cy is None or v[1] == cy)
    ]


def add_all(terms):
    terms = list(terms)
    while len(terms) > 1:
        terms = [
            terms[k] + terms[k + 1] if k + 1 < len(terms) else terms[k]
            for k in range(0, len(terms), 2)
        ]
    return terms[0]


def along(values, axis):
    total = None
    for vel, val in zip(PAIRS, values):
        if vel[axis] == 0:
            continue
        if total is None:
            total = val if vel[axis] > 0 else -val
        else:
            total = total + val if vel[axis] > 0 else total - val
    return total


def dotted(vec, vel):
    total = None
    for comp, c in zip(vec, vel):
        if c == 0:
            continue
        if total is None:
            total = comp if c > 0 else -comp
        else:
            total = total + comp if c > 0 else total - comp
    return total


def adjoint_cell(f, a, blocking):
    fe = [f[2 * k + 1] + f[2 * k + 2] for k in range(9)]
    fo = [f[2 * k + 1] - f[2 * k + 2] for k in range(9)]
    rho = add_all([f[0]] + fe)
    inv = 1.0 / rho
    u = [along(fo, d) * inv for d in range(3)]
    usq = u[0] * u[0] + u[1] * u[1] + u[2] * u[2]

    e = [a[2 * k + 1] + a[2 * k + 2] for k in range(9)]
    o = [a[2 * k + 1] - a[2 * k + 2] for k in range(9)]
    mom = [0.28 * along(o, d) for d in range(3)]
    big_o = [1.4 * o[k] - dotted(mom, PAIRS[k]) for k in range(9)]
    edge = [e[3] + e[4], e[5] + e[6], e[7] + e[8]]
    axis_sum = e[0] + e[1] + e[2]
    edge_sum = edge[0] + edge[1] + edge[2]
    mean16 = (1.6 / 19.0) * (a[0] + axis_sum + edge_sum)
    a4 = 4.0 * a[0]
    t = [
        edge[0] - 2.0 * (e[0] + e[1]) + a4,
        edge[1] - 2.0 * (e[0] + e[2]) + a4,
        edge[2] - 2.0 * (e[1] + e[2]) + a4,
    ]
    tsum = (2.0 / 7.0) * (t[0] + t[1] + t[2])
    p = [(0.4 / 12.0) * (tk - tsum) for tk in t]
    b0 = 1.6 * a[0] - mean16 - 4.0 * (p[0] + p[1] + p[2])
    q = [-2.0 * (p[0] + p[1]), -2.0 * (p[0] + p[2]), -2.0 * (p[1] + p[2])]
    shift = [2.0 * (mean16 + val) for val in q + p]
    plane = [0, 1, 2, 3, 3, 4, 4, 5, 5]
    big_e = [1.6 * e[k] - shift[plane[k]] for k in range(9)]

    c36 = 1.0 / 36.0
    s3, s5, s7 = big_e[3] + big_e[4], big_e[5] + big_e[6], big_e[7] + big_e[8]
    zeroth = (1.0 / 3.0) * b0 + c36 * (
        2.0 * (big_e[0] + big_e[1] + big_e[2]) + s3 + s5 + s7
    )
    xx = c36 * (2.0 * big_e[0] + s3 + s5)
    yy = c36 * (2.0 * big_e[1] + s3 + s7)
    zz = c36 * (2.0 * big_e[2] + s5 + s7)
    xy = c36 * (big_e[3] - big_e[4])
    xz = c36 * (big_e[5] - big_e[6])
    yz = c36 * (big_e[7] - big_e[8])
    weighted = [2.0 * big_o[k] if k < 3 else big_o[k] for k in range(9)]
    first = [c36 * along(weighted, d) for d in range(3)]
    bu = [
        xx * u[0] + xy * u[1] + xz * u[2],
        xy * u[0] + yy * u[1] + yz * u[2],
        xz * u[0] + yz * u[1] + zz * u[2],
    ]
    ubu = 4.5 * (u[0] * bu[0] + u[1] * bu[1] + u[2] * bu[2])
    half_u = 1.5 * usq * zeroth
    scalar = zeroth + half_u - ubu
    vec = [3.0 * (first[d] - zeroth * u[d]) + 9.0 * bu[d] for d in range(3)]
    eq_b = zeroth - half_u + ubu + 3.0 * (
        first[0] * u[0] + first[1] * u[1] + first[2] * u[2]
    )

    open_part = 1.0 - blocking
    odd_keep = 1.0 - 2.0 * blocking
    result = [None] * 19
    result[0] = a[0] + open_part * (scalar - b0)
    half_open = 0.5 * open_part
    half_keep = 0.5 * odd_keep
    scalar2 = 2.0 * scalar
    vec2 = [2.0 * val for val in vec]
    for k in range(9):
        even = 0.5 * e[k] + half_open * (scalar2 - big_e[k])
        odd = half_keep * o[k] + half_open * (dotted(vec2, PAIRS[k]) - big_o[k])
        result[2 * k + 1] = even + odd
        result[2 * k + 2] = even - odd
    parts = [b0 * f[0] - rho * eq_b]
    for k in range(9):
        parts.append(0.5 * (big_e[k] * fe[k] + big_o[k] * fo[k]) - fo[k] * o[k])
    return result, add_all(parts)


def kernel(
    nx,
    ny,
    adj_hbm,
    pops_hbm,
    solid_hbm,
    label_hbm,
    design_hbm,
    out_ref,
    sens_ref,
    adj,
    pops,
    solid,
    label,
    design,
    mid,
    pull,
    send1,
    recv1,
    send2,
    recv2,
    send3,
    recv3,
    gath,
    part,
    in_sem,
    s_sem,
    r_sem,
    gs_sem,
    gr_sem,
):
    mx, my = lax.axis_index("gx"), lax.axis_index("gy")

    def has(d):
        conds = []
        if d[0] < 0:
            conds.append(mx > 0)
        if d[0] > 0:
            conds.append(mx < nx - 1)
        if d[1] < 0:
            conds.append(my > 0)
        if d[1] > 0:
            conds.append(my < ny - 1)
        return functools.reduce(jnp.logical_and, conds)

    barrier = pltpu.get_barrier_semaphore()
    count = nx * ny
    mine = mx * ny + my

    def peer(k):
        flat = lax.rem(mine + k, count)
        return (flat // ny, lax.rem(flat, ny))

    def each_peer(body):
        if count <= 64:
            for k in range(1, count):
                body(k)
        else:

            @pl.loop(1, count)
            def _(k):
                body(k)

    @each_peer
    def _(k):
        pl.semaphore_signal(barrier, inc=1, device_id=peer(k), device_id_type=MESH)

    loads = [
        pltpu.make_async_copy(src, dst, in_sem.at[k])
        for k, (src, dst) in enumerate(
            [
                (adj_hbm, adj),
                (label_hbm, label),
                (pops_hbm, pops),
                (solid_hbm, solid),
                (design_hbm, design),
            ]
        )
    ]
    for load in loads:
        load.start()

    for n, d in enumerate(DIRS):

        @pl.when(jnp.logical_not(has((-d[0], -d[1]))))
        def _():
            for buf in (recv1, recv2, recv3):
                buf[n] = jnp.zeros(buf.shape[1:], F32)

    lane = lax.broadcasted_iota(jnp.int32, (16, 128), 1)
    lane4 = lax.broadcasted_iota(jnp.int32, (4, 128), 1)

    def copies(rnd, send, recv):
        out = []
        for n, d in enumerate(DIRS):
            rows = {0: (32, 16, 16), 1: (24, 16, 8), 2: (8, 16, 8)}[rnd][
                0 if d[1] == 0 else (1 if d[0] == 0 else 2)
            ]
            start = 0
            if rnd == 2 and d[0] > 0:
                start = 8
            src = send.at[pl.ds(start, rows)] if rnd == 2 else send.at[n, pl.ds(0, rows)]
            out.append(
                pltpu.make_async_remote_copy(
                    src_ref=src,
                    dst_ref=recv.at[n, pl.ds(0, rows)],
                    send_sem=s_sem.at[rnd, n],
                    recv_sem=r_sem.at[rnd, n],
                    device_id=(mx + d[0], my + d[1]),
                    device_id_type=MESH,
                )
            )
        return out

    def start_all(cps):
        for n, d in enumerate(DIRS):

            @pl.when(has(d))
            def _():
                cps[n].start()

    def recv_all(cps):
        for n, d in enumerate(DIRS):

            @pl.when(has((-d[0], -d[1])))
            def _():
                cps[n].wait_recv()

    def send_done(cps):
        for n, d in enumerate(DIRS):

            @pl.when(has(d))
            def _():
                cps[n].wait_send()

    def pack(src, send, region):
        for n, (dx, dy) in enumerate(DIRS):
            if dy == 0:
                row = 0 if dx < 0 else 15
                for j, i in enumerate(pops_with(cx=-dx)):
                    for z in range(4):
                        send[n, 4 * j + z : 4 * j + z + 1] = src[i, z, row : row + 1, :]
                if region is not None:
                    send[n, 24:32] = region[0:8] if dx < 0 else region[8:16]
            elif dx == 0:
                at = 0 if dy < 0 else 127
                base = 64 if dy < 0 else 0
                acc = region if region is not None else jnp.zeros((16, 128), F32)
                for j, i in enumerate(pops_with(cy=-dy)):
                    for z in range(4):
                        to = base + 4 * j + z
                        moved = pltpu.roll(src[i, z], (to - at) % 128, 1)
                        acc = jnp.where(lane == to, moved, acc)
                send[n, 0:16] = acc
            else:
                row = 0 if dx < 0 else 15
                i = VELOCITIES.index((-dx, -dy, 0))
                for z in range(4):
                    send[n, z : z + 1] = src[i, z, row : row + 1, :]
                if region is not None:
                    send[n, 8:16] = region[0:8] if dx < 0 else region[8:16]

    def pull_local(src):
        for i, (cx, cy, cz) in enumerate(VELOCITIES):
            for z in range(4):
                val = src[i, z]
                if cy != 0:
                    val = pltpu.roll(val, (-cy) % 128, 1)
                pull[i, z, 8:24] = val

    def pull_edges(recv):
        for n, (dx, dy) in enumerate(DIRS):
            if dx == 0:
                base = 64 if dy < 0 else 0
                at = 127 if dy < 0 else 0
                got = recv[n, 0:16]
                for j, i in enumerate(pops_with(cy=-dy)):
                    for z in range(4):
                        moved = pltpu.roll(got, (at - base - 4 * j - z) % 128, 1)
                        pull[i, z, 8:24] = jnp.where(lane == at, moved, pull[i, z, 8:24])
            elif dy == 0:
                row = 24 if dx < 0 else 7
                for j, i in enumerate(pops_with(cx=-dx)):
                    cy = VELOCITIES[i][1]
                    val = recv[n, 4 * j : 4 * j + 4]
                    if cy != 0:
                        val = pltpu.roll(val, (-cy) % 128, 1)
                        corner = recv[DIRS.index((dx, -cy)), 0:4]
                        corner = pltpu.roll(corner, (-cy) % 128, 1)
                        val = jnp.where(lane4 == (127 if cy > 0 else 0), corner, val)
                    for z in range(4):
                        pull[i, z, row : row + 1] = val[z : z + 1]

    def cells(section, dst):
        total = None
        for z in range(4):
            f = [pops[section, i, z].astype(F32) for i in range(19)]
            a = []
            for i, (cx, cy, cz) in enumerate(VELOCITIES):
                a.append(pull[i, (z + cz) % 4, 8 + cx : 24 + cx, :])
            is_solid = solid[z] == 1
            inside = label[...] > 0
            blocking = jnp.where(
                is_solid, 1.0, jnp.where(inside, BLOCK_LIMIT * design[...], 0.0)
            )
            lever = jnp.where(
                jnp.logical_and(jnp.logical_not(is_solid), inside), BLOCK_LIMIT, 0.0
            )
            result, term = adjoint_cell(f, a, blocking)
            for i in range(19):
                dst[i, z] = result[i]
            term = term * lever
            total = term if total is None else total + term
        return total

    wide_row = lax.broadcasted_iota(jnp.int32, (32, 256), 0)
    wide_lane = lax.broadcasted_iota(jnp.int32, (32, 256), 1)
    gone = jnp.logical_or(
        jnp.logical_or(
            jnp.logical_and(wide_row >= 24, mx == 0),
            jnp.logical_and(
                jnp.logical_and(wide_row >= 16, wide_row < 24), mx == nx - 1
            ),
        ),
        jnp.logical_or(
            jnp.logical_and(wide_lane >= 192, my == 0),
            jnp.logical_and(
                jnp.logical_and(wide_lane >= 128, wide_lane < 192), my == ny - 1
            ),
        ),
    )
    scale_den = 1.0 / (1.0 + 4.0 * FILTER_WEIGHT)
    keep = jnp.where(gone, 0.0, scale_den)

    def widened(own, get):
        low = lane[0:8] < 64
        top = jnp.concatenate(
            [own, jnp.where(lane < 64, get((0, -1)), get((0, 1)))], axis=1
        )
        down = jnp.concatenate(
            [get((-1, 0)), jnp.where(low, get((-1, -1)), get((-1, 1)))], axis=1
        )
        up = jnp.concatenate(
            [get((1, 0)), jnp.where(low, get((1, -1)), get((1, 1)))], axis=1
        )
        return jnp.concatenate([top, down, up], axis=0)

    def jacobi(start):
        base = start * keep
        weight = FILTER_WEIGHT * keep
        smooth = jnp.where(gone, 0.0, start)
        for _ in range(SWEEPS):
            beside = (
                pltpu.roll(smooth, 1, 0)
                + pltpu.roll(smooth, 31, 0)
                + pltpu.roll(smooth, 1, 1)
                + pltpu.roll(smooth, 255, 1)
            )
            smooth = base + weight * beside
        return smooth

    loads[0].wait()
    loads[1].wait()
    region = label[...].astype(F32)
    pack(adj, send1, region)
    pl.semaphore_wait(barrier, count - 1)
    cps1 = copies(0, send1, recv1)
    start_all(cps1)
    pull_local(adj)
    for load in loads[2:]:
        load.wait()
    recv_all(cps1)
    pull_edges(recv1)
    raw1 = cells(1, mid)

    pack(mid, send2, None)
    cps2 = copies(1, send2, recv2)
    start_all(cps2)
    pull_local(mid)

    def label_of(d):
        n = DIRS.index(d)
        if d[1] == 0:
            return recv1[n, 24:32]
        if d[0] == 0:
            return recv1[n, 0:16]
        return recv1[n, 8:16]

    wide_label = widened(region, label_of)
    share = []
    for r in (1.0, 2.0):
        share.append(jacobi(jnp.where(wide_label == r, 1.0, 0.0))[0:16, 0:128])

    quarter = lax.broadcasted_iota(jnp.int32, (1, 128), 1) // 32

    def folded(vals):
        row = jnp.zeros((1, 128), F32)
        for k, val in enumerate(vals):
            val = jnp.sum(val, axis=0, keepdims=True)
            val = val + pltpu.roll(val, 64, 1)
            val = val + pltpu.roll(val, 32, 1)
            row = jnp.where(quarter == k, val, row)
        return row

    zero = jnp.zeros((16, 128), F32)
    counts = folded(
        [zero, zero, jnp.where(region == 1.0, 1.0, 0.0), jnp.where(region == 2.0, 1.0, 0.0)]
    )

    recv_all(cps2)
    pull_edges(recv2)
    raw2 = cells(0, out_ref)
    raw = SENSE_SCALE * (raw1 + raw2)
    send3[...] = raw

    cps3 = copies(2, send3, recv3)
    start_all(cps3)
    own_sums = folded([raw * share[0], raw * share[1]]) + counts
    part[...] = own_sums

    def sums_to(k):
        return pltpu.make_async_remote_copy(
            src_ref=part,
            dst_ref=gath.at[k - 1],
            send_sem=gs_sem.at[k - 1],
            recv_sem=gr_sem.at[k - 1],
            device_id=peer(k),
            device_id_type=MESH,
        )

    @each_peer
    def _(k):
        sums_to(k).start()

    recv_all(cps3)

    def raw_of(d):
        n = DIRS.index(d)
        return recv3[n, 0:16] if d[0] == 0 else recv3[n, 0:8]

    smooth = jacobi(widened(raw, raw_of))[0:16, 0:128]

    @each_peer
    def _(k):
        sums_to(k).wait_recv()

    total = own_sums + jnp.sum(gath[...], axis=0)
    tot = [
        jnp.sum(jnp.where(quarter == k, total, 0.0), axis=1, keepdims=True) for k in range(4)
    ]
    mean1 = tot[0] / jnp.maximum(tot[2], 1.0)
    mean2 = tot[1] / jnp.maximum(tot[3], 1.0)
    sens_ref[...] = jnp.where(
        region == 1.0, smooth - mean1, jnp.where(region == 2.0, smooth - mean2, 0.0)
    )
    send_done(cps1)
    send_done(cps2)
    send_done(cps3)

    @each_peer
    def _(k):
        sums_to(k).wait_send()


def per_device(nx, ny, adjoint_in, forward_pops, solid_mask, region_label, design):
    vmem, dma = pltpu.VMEM, pltpu.SemaphoreType.DMA
    return pl.pallas_call(
        functools.partial(kernel, nx, ny),
        out_shape=(
            jax.ShapeDtypeStruct(adjoint_in.shape, F32),
            jax.ShapeDtypeStruct(design.shape, F32),
        ),
        in_specs=[pl.BlockSpec(memory_space=pltpu.HBM)] * 5,
        out_specs=(
            pl.BlockSpec(memory_space=pltpu.VMEM),
            pl.BlockSpec(memory_space=pltpu.VMEM),
        ),
        scratch_shapes=[
            vmem(adjoint_in.shape, F32),
            vmem(forward_pops.shape, jnp.bfloat16),
            vmem(solid_mask.shape, jnp.int32),
            vmem(region_label.shape, jnp.int32),
            vmem(design.shape, F32),
            vmem(adjoint_in.shape, F32),
            vmem((19, 4, 32, 128), F32),
            vmem((8, 32, 128), F32),
            vmem((8, 32, 128), F32),
            vmem((8, 24, 128), F32),
            vmem((8, 24, 128), F32),
            vmem((16, 128), F32),
            vmem((8, 16, 128), F32),
            vmem((nx * ny - 1, 1, 128), F32),
            vmem((1, 128), F32),
            dma((5,)),
            dma((3, 8)),
            dma((3, 8)),
            dma((nx * ny - 1,)),
            dma((nx * ny - 1,)),
        ],
        compiler_params=pltpu.CompilerParams(
            collective_id=0, has_side_effects=True, vmem_limit_bytes=40 * 1024 * 1024
        ),
    )(
        *(
            pltpu.with_memory_space_constraint(arg, pltpu.HBM)
            for arg in (adjoint_in, forward_pops, solid_mask, region_label, design)
        )
    )


def solution(mesh):
    in_specs = (
        P(None, None, "gx", "gy"),
        P(None, None, None, "gx", "gy"),
        P(None, "gx", "gy"),
        P("gx", "gy"),
        P("gx", "gy"),
    )
    out_specs = (P(None, None, "gx", "gy"), P("gx", "gy"))
    return jax.shard_map(
        functools.partial(per_device, mesh.shape["gx"], mesh.shape["gy"]),
        mesh=mesh,
        in_specs=in_specs,
        out_specs=out_specs,
        check_vma=False,
    )
```

```python
import functools

import jax
import jax.numpy as jnp
from jax import lax
from jax.experimental import pallas as pl
from jax.experimental.pallas import tpu as pltpu
from jax.sharding import PartitionSpec as P

SWEEPS = 4
VELOCITIES = [
    (0, 0, 0),
    (1, 0, 0),
    (-1, 0, 0),
    (0, 1, 0),
    (0, -1, 0),
    (0, 0, 1),
    (0, 0, -1),
    (1, 1, 0),
    (-1, -1, 0),
    (1, -1, 0),
    (-1, 1, 0),
    (1, 0, 1),
    (-1, 0, -1),
    (1, 0, -1),
    (-1, 0, 1),
    (0, 1, 1),
    (0, -1, -1),
    (0, 1, -1),
    (0, -1, 1),
]
PAIRS = [VELOCITIES[2 * k + 1] for k in range(9)]
BLOCK_LIMIT = 0.5
SENSE_SCALE = 20.0
FILTER_WEIGHT = 16.0
MESH = pl.DeviceIdType.MESH
F32 = jnp.float32

DIRS = [(-1, 0), (1, 0), (0, -1), (0, 1), (-1, -1), (-1, 1), (1, -1), (1, 1)]


def pops_with(cx=None, cy=None):
    return [
        i
        for i, v in enumerate(VELOCITIES)
        if (cx is None or v[0] == cx) and (cy is None or v[1] == cy)
    ]


def add_all(terms):
    terms = list(terms)
    while len(terms) > 1:
        terms = [
            terms[k] + terms[k + 1] if k + 1 < len(terms) else terms[k]
            for k in range(0, len(terms), 2)
        ]
    return terms[0]


def along(values, axis):
    total = None
    for vel, val in zip(PAIRS, values):
        if vel[axis] == 0:
            continue
        if total is None:
            total = val if vel[axis] > 0 else -val
        else:
            total = total + val if vel[axis] > 0 else total - val
    return total


def dotted(vec, vel):
    total = None
    for comp, c in zip(vec, vel):
        if c == 0:
            continue
        if total is None:
            total = comp if c > 0 else -comp
        else:
            total = total + comp if c > 0 else total - comp
    return total


def adjoint_cell(f, a, blocking):
    fe = [f[2 * k + 1] + f[2 * k + 2] for k in range(9)]
    fo = [f[2 * k + 1] - f[2 * k + 2] for k in range(9)]
    rho = add_all([f[0]] + fe)
    inv = 1.0 / rho
    u = [along(fo, d) * inv for d in range(3)]
    usq = u[0] * u[0] + u[1] * u[1] + u[2] * u[2]

    e = [a[2 * k + 1] + a[2 * k + 2] for k in range(9)]
    o = [a[2 * k + 1] - a[2 * k + 2] for k in range(9)]
    mom = [0.28 * along(o, d) for d in range(3)]
    big_o = [1.4 * o[k] - dotted(mom, PAIRS[k]) for k in range(9)]
    edge = [e[3] + e[4], e[5] + e[6], e[7] + e[8]]
    axis_sum = e[0] + e[1] + e[2]
    edge_sum = edge[0] + edge[1] + edge[2]
    mean16 = (1.6 / 19.0) * (a[0] + axis_sum + edge_sum)
    a4 = 4.0 * a[0]
    t = [
        edge[0] - 2.0 * (e[0] + e[1]) + a4,
        edge[1] - 2.0 * (e[0] + e[2]) + a4,
        edge[2] - 2.0 * (e[1] + e[2]) + a4,
    ]
    tsum = (2.0 / 7.0) * (t[0] + t[1] + t[2])
    p = [(0.4 / 12.0) * (tk - tsum) for tk in t]
    b0 = 1.6 * a[0] - mean16 - 4.0 * (p[0] + p[1] + p[2])
    q = [-2.0 * (p[0] + p[1]), -2.0 * (p[0] + p[2]), -2.0 * (p[1] + p[2])]
    shift = [2.0 * (mean16 + val) for val in q + p]
    plane = [0, 1, 2, 3, 3, 4, 4, 5, 5]
    big_e = [1.6 * e[k] - shift[plane[k]] for k in range(9)]

    c36 = 1.0 / 36.0
    s3, s5, s7 = big_e[3] + big_e[4], big_e[5] + big_e[6], big_e[7] + big_e[8]
    zeroth = (1.0 / 3.0) * b0 + c36 * (
        2.0 * (big_e[0] + big_e[1] + big_e[2]) + s3 + s5 + s7
    )
    xx = c36 * (2.0 * big_e[0] + s3 + s5)
    yy = c36 * (2.0 * big_e[1] + s3 + s7)
    zz = c36 * (2.0 * big_e[2] + s5 + s7)
    xy = c36 * (big_e[3] - big_e[4])
    xz = c36 * (big_e[5] - big_e[6])
    yz = c36 * (big_e[7] - big_e[8])
    weighted = [2.0 * big_o[k] if k < 3 else big_o[k] for k in range(9)]
    first = [c36 * along(weighted, d) for d in range(3)]
    bu = [
        xx * u[0] + xy * u[1] + xz * u[2],
        xy * u[0] + yy * u[1] + yz * u[2],
        xz * u[0] + yz * u[1] + zz * u[2],
    ]
    ubu = 4.5 * (u[0] * bu[0] + u[1] * bu[1] + u[2] * bu[2])
    half_u = 1.5 * usq * zeroth
    scalar = zeroth + half_u - ubu
    vec = [3.0 * (first[d] - zeroth * u[d]) + 9.0 * bu[d] for d in range(3)]
    eq_b = zeroth - half_u + ubu + 3.0 * (
        first[0] * u[0] + first[1] * u[1] + first[2] * u[2]
    )

    open_part = 1.0 - blocking
    odd_keep = 1.0 - 2.0 * blocking
    result = [None] * 19
    result[0] = a[0] + open_part * (scalar - b0)
    half_open = 0.5 * open_part
    half_keep = 0.5 * odd_keep
    scalar2 = 2.0 * scalar
    vec2 = [2.0 * val for val in vec]
    for k in range(9):
        even = 0.5 * e[k] + half_open * (scalar2 - big_e[k])
        odd = half_keep * o[k] + half_open * (dotted(vec2, PAIRS[k]) - big_o[k])
        result[2 * k + 1] = even + odd
        result[2 * k + 2] = even - odd
    parts = [b0 * f[0] - rho * eq_b]
    for k in range(9):
        parts.append(0.5 * (big_e[k] * fe[k] + big_o[k] * fo[k]) - fo[k] * o[k])
    return result, add_all(parts)


def kernel(
    nx,
    ny,
    adj_hbm,
    pops_hbm,
    solid_hbm,
    label_hbm,
    design_hbm,
    out_ref,
    sens_ref,
    adj,
    pops,
    solid,
    label,
    design,
    mid,
    pull,
    send1,
    recv1,
    send2,
    recv2,
    send3,
    recv3,
    gath,
    part,
    in_sem,
    s_sem,
    r_sem,
    gs_sem,
    gr_sem,
):
    mx, my = lax.axis_index("gx"), lax.axis_index("gy")

    def has(d):
        conds = []
        if d[0] < 0:
            conds.append(mx > 0)
        if d[0] > 0:
            conds.append(mx < nx - 1)
        if d[1] < 0:
            conds.append(my > 0)
        if d[1] > 0:
            conds.append(my < ny - 1)
        return functools.reduce(jnp.logical_and, conds)

    barrier = pltpu.get_barrier_semaphore()
    count = nx * ny
    mine = mx * ny + my

    loads = [
        pltpu.make_async_copy(src, dst, in_sem.at[k])
        for k, (src, dst) in enumerate(
            [
                (label_hbm, label),
                (adj_hbm.at[pl.ds(0, 7)], adj.at[pl.ds(0, 7)]),
                (adj_hbm.at[pl.ds(7, 6)], adj.at[pl.ds(7, 6)]),
                (adj_hbm.at[pl.ds(13, 6)], adj.at[pl.ds(13, 6)]),
                (pops_hbm, pops),
                (solid_hbm, solid),
                (design_hbm, design),
            ]
        )
    ]
    for load in loads:
        load.start()

    def wrapped(pos, step, size):
        to = pos + step
        return jnp.where(to >= size, to - size, to)

    peer_x = [wrapped(mx, k, nx) for k in range(nx)]
    peer_y = [wrapped(my, k, ny) for k in range(ny)]

    def each_peer(body):
        if count <= 64:
            for k in range(1, count):
                body(k, (peer_x[k // ny], peer_y[k % ny]))
        else:

            @pl.loop(1, count)
            def _(k):
                body(k, (wrapped(mx, k // ny, nx), wrapped(my, lax.rem(k, ny), ny)))

    @each_peer
    def _(k, peer):
        pl.semaphore_signal(barrier, inc=1, device_id=peer, device_id_type=MESH)

    for n, d in enumerate(DIRS):

        @pl.when(jnp.logical_not(has((-d[0], -d[1]))))
        def _():
            for buf in (recv1, recv2, recv3):
                buf[n] = jnp.zeros(buf.shape[1:], F32)

    lane = lax.broadcasted_iota(jnp.int32, (16, 128), 1)
    lane4 = lax.broadcasted_iota(jnp.int32, (4, 128), 1)

    def copies(rnd, send, recv):
        out = []
        for n, d in enumerate(DIRS):
            rows = {0: (32, 16, 16), 1: (24, 16, 8), 2: (8, 16, 8)}[rnd][
                0 if d[1] == 0 else (1 if d[0] == 0 else 2)
            ]
            start = 0
            if rnd == 2 and d[0] > 0:
                start = 8
            src = send.at[pl.ds(start, rows)] if rnd == 2 else send.at[n, pl.ds(0, rows)]
            out.append(
                pltpu.make_async_remote_copy(
                    src_ref=src,
                    dst_ref=recv.at[n, pl.ds(0, rows)],
                    send_sem=s_sem.at[rnd, n],
                    recv_sem=r_sem.at[rnd, n],
                    device_id=(mx + d[0], my + d[1]),
                    device_id_type=MESH,
                )
            )
        return out

    def start_all(cps):
        for n, d in enumerate(DIRS):

            @pl.when(has(d))
            def _():
                cps[n].start()

    def recv_all(cps):
        for n, d in enumerate(DIRS):

            @pl.when(has((-d[0], -d[1])))
            def _():
                cps[n].wait_recv()

    def send_done(cps):
        for n, d in enumerate(DIRS):

            @pl.when(has(d))
            def _():
                cps[n].wait_send()

    def pack(src, send, region):
        for n, (dx, dy) in enumerate(DIRS):
            if dy == 0:
                row = 0 if dx < 0 else 15
                for j, i in enumerate(pops_with(cx=-dx)):
                    for z in range(4):
                        send[n, 4 * j + z : 4 * j + z + 1] = src[i, z, row : row + 1, :]
                if region is not None:
                    send[n, 24:32] = region[0:8] if dx < 0 else region[8:16]
            elif dx == 0:
                at = 0 if dy < 0 else 127
                base = 64 if dy < 0 else 0
                acc = region if region is not None else jnp.zeros((16, 128), F32)
                for j, i in enumerate(pops_with(cy=-dy)):
                    for z in range(4):
                        to = base + 4 * j + z
                        moved = pltpu.roll(src[i, z], (to - at) % 128, 1)
                        acc = jnp.where(lane == to, moved, acc)
                send[n, 0:16] = acc
            else:
                row = 0 if dx < 0 else 15
                i = VELOCITIES.index((-dx, -dy, 0))
                for z in range(4):
                    send[n, z : z + 1] = src[i, z, row : row + 1, :]
                if region is not None:
                    send[n, 8:16] = region[0:8] if dx < 0 else region[8:16]

    def pull_local(src):
        for i, (cx, cy, cz) in enumerate(VELOCITIES):
            for z in range(4):
                val = src[i, z]
                if cy != 0:
                    val = pltpu.roll(val, (-cy) % 128, 1)
                pull[i, z, 8:24] = val

    def pull_edges(recv):
        for n, (dx, dy) in enumerate(DIRS):
            if dx == 0:
                base = 64 if dy < 0 else 0
                at = 127 if dy < 0 else 0
                got = recv[n, 0:16]
                for j, i in enumerate(pops_with(cy=-dy)):
                    for z in range(4):
                        moved = pltpu.roll(got, (at - base - 4 * j - z) % 128, 1)
                        pull[i, z, 8:24] = jnp.where(lane == at, moved, pull[i, z, 8:24])
            elif dy == 0:
                row = 24 if dx < 0 else 7
                for j, i in enumerate(pops_with(cx=-dx)):
                    cy = VELOCITIES[i][1]
                    val = recv[n, 4 * j : 4 * j + 4]
                    if cy != 0:
                        val = pltpu.roll(val, (-cy) % 128, 1)
                        corner = recv[DIRS.index((dx, -cy)), 0:4]
                        corner = pltpu.roll(corner, (-cy) % 128, 1)
                        val = jnp.where(lane4 == (127 if cy > 0 else 0), corner, val)
                    for z in range(4):
                        pull[i, z, row : row + 1] = val[z : z + 1]

    def cells(section, dst):
        total = None
        for z in range(4):
            f = [pops[section, i, z].astype(F32) for i in range(19)]
            a = []
            for i, (cx, cy, cz) in enumerate(VELOCITIES):
                a.append(pull[i, (z + cz) % 4, 8 + cx : 24 + cx, :])
            is_solid = solid[z] == 1
            inside = label[...] > 0
            blocking = jnp.where(
                is_solid, 1.0, jnp.where(inside, BLOCK_LIMIT * design[...], 0.0)
            )
            lever = jnp.where(
                jnp.logical_and(jnp.logical_not(is_solid), inside), BLOCK_LIMIT, 0.0
            )
            result, term = adjoint_cell(f, a, blocking)
            for i in range(19):
                dst[i, z] = result[i]
            term = term * lever
            total = term if total is None else total + term
        return total

    wide_row = lax.broadcasted_iota(jnp.int32, (32, 256), 0)
    wide_lane = lax.broadcasted_iota(jnp.int32, (32, 256), 1)
    gone = jnp.logical_or(
        jnp.logical_or(
            jnp.logical_and(wide_row >= 24, mx == 0),
            jnp.logical_and(
                jnp.logical_and(wide_row >= 16, wide_row < 24), mx == nx - 1
            ),
        ),
        jnp.logical_or(
            jnp.logical_and(wide_lane >= 192, my == 0),
            jnp.logical_and(
                jnp.logical_and(wide_lane >= 128, wide_lane < 192), my == ny - 1
            ),
        ),
    )
    scale_den = 1.0 / (1.0 + 4.0 * FILTER_WEIGHT)
    keep = jnp.where(gone, 0.0, scale_den)

    def widened(own, get):
        low = lane[0:8] < 64
        top = jnp.concatenate(
            [own, jnp.where(lane < 64, get((0, -1)), get((0, 1)))], axis=1
        )
        down = jnp.concatenate(
            [get((-1, 0)), jnp.where(low, get((-1, -1)), get((-1, 1)))], axis=1
        )
        up = jnp.concatenate(
            [get((1, 0)), jnp.where(low, get((1, -1)), get((1, 1)))], axis=1
        )
        return jnp.concatenate([top, down, up], axis=0)

    def jacobi(start):
        base = start * keep
        weight = FILTER_WEIGHT * keep
        smooth = jnp.where(gone, 0.0, start)
        for _ in range(SWEEPS):
            beside = (
                pltpu.roll(smooth, 1, 0)
                + pltpu.roll(smooth, 31, 0)
                + pltpu.roll(smooth, 1, 1)
                + pltpu.roll(smooth, 255, 1)
            )
            smooth = base + weight * beside
        return smooth

    for load in loads[:4]:
        load.wait()
    region = label[...].astype(F32)
    pack(adj, send1, region)
    pl.semaphore_wait(barrier, count - 1)
    cps1 = copies(0, send1, recv1)
    start_all(cps1)
    pull_local(adj)
    for load in loads[4:]:
        load.wait()
    recv_all(cps1)
    pull_edges(recv1)
    raw1 = cells(1, mid)

    pack(mid, send2, None)
    cps2 = copies(1, send2, recv2)
    start_all(cps2)
    pull_local(mid)

    def label_of(d):
        n = DIRS.index(d)
        if d[1] == 0:
            return recv1[n, 24:32]
        if d[0] == 0:
            return recv1[n, 0:16]
        return recv1[n, 8:16]

    wide_label = widened(region, label_of)
    share = []
    for r in (1.0, 2.0):
        share.append(jacobi(jnp.where(wide_label == r, 1.0, 0.0))[0:16, 0:128])

    quarter = lax.broadcasted_iota(jnp.int32, (1, 128), 1) // 32

    def folded(vals):
        row = jnp.zeros((1, 128), F32)
        for k, val in enumerate(vals):
            val = jnp.sum(val, axis=0, keepdims=True)
            val = val + pltpu.roll(val, 64, 1)
            val = val + pltpu.roll(val, 32, 1)
            row = jnp.where(quarter == k, val, row)
        return row

    zero = jnp.zeros((16, 128), F32)
    counts = folded(
        [zero, zero, jnp.where(region == 1.0, 1.0, 0.0), jnp.where(region == 2.0, 1.0, 0.0)]
    )

    recv_all(cps2)
    pull_edges(recv2)
    raw2 = cells(0, out_ref)
    raw = SENSE_SCALE * (raw1 + raw2)
    send3[...] = raw

    cps3 = copies(2, send3, recv3)
    start_all(cps3)
    own_sums = folded([raw * share[0], raw * share[1]]) + counts
    part[...] = own_sums

    @each_peer
    def _(k, peer):
        pltpu.make_async_remote_copy(
            src_ref=part,
            dst_ref=gath.at[k - 1],
            send_sem=gs_sem.at[0],
            recv_sem=gr_sem.at[0],
            device_id=peer,
            device_id_type=MESH,
        ).start()

    send_done(cps1)
    send_done(cps2)
    recv_all(cps3)

    def raw_of(d):
        n = DIRS.index(d)
        return recv3[n, 0:16] if d[0] == 0 else recv3[n, 0:8]

    smooth = jacobi(widened(raw, raw_of))[0:16, 0:128]

    send_done(cps3)
    pltpu.make_async_copy(gath, gath, gs_sem.at[0]).wait()
    pltpu.make_async_copy(gath, gath, gr_sem.at[0]).wait()
    total = own_sums + jnp.sum(gath[...], axis=0)
    tot = [
        jnp.sum(jnp.where(quarter == k, total, 0.0), axis=1, keepdims=True) for k in range(4)
    ]
    mean1 = tot[0] / jnp.maximum(tot[2], 1.0)
    mean2 = tot[1] / jnp.maximum(tot[3], 1.0)
    sens_ref[...] = jnp.where(
        region == 1.0, smooth - mean1, jnp.where(region == 2.0, smooth - mean2, 0.0)
    )


def per_device(nx, ny, adjoint_in, forward_pops, solid_mask, region_label, design):
    vmem, dma = pltpu.VMEM, pltpu.SemaphoreType.DMA
    return pl.pallas_call(
        functools.partial(kernel, nx, ny),
        out_shape=(
            jax.ShapeDtypeStruct(adjoint_in.shape, F32),
            jax.ShapeDtypeStruct(design.shape, F32),
        ),
        in_specs=[pl.BlockSpec(memory_space=pltpu.HBM)] * 5,
        out_specs=(
            pl.BlockSpec(memory_space=pltpu.VMEM),
            pl.BlockSpec(memory_space=pltpu.VMEM),
        ),
        scratch_shapes=[
            vmem(adjoint_in.shape, F32),
            vmem(forward_pops.shape, jnp.bfloat16),
            vmem(solid_mask.shape, jnp.int32),
            vmem(region_label.shape, jnp.int32),
            vmem(design.shape, F32),
            vmem(adjoint_in.shape, F32),
            vmem((19, 4, 32, 128), F32),
            vmem((8, 32, 128), F32),
            vmem((8, 32, 128), F32),
            vmem((8, 24, 128), F32),
            vmem((8, 24, 128), F32),
            vmem((16, 128), F32),
            vmem((8, 16, 128), F32),
            vmem((nx * ny - 1, 1, 128), F32),
            vmem((1, 128), F32),
            dma((7,)),
            dma((3, 8)),
            dma((3, 8)),
            dma((1,)),
            dma((1,)),
        ],
        compiler_params=pltpu.CompilerParams(
            collective_id=0, has_side_effects=True, vmem_limit_bytes=40 * 1024 * 1024
        ),
    )(
        *(
            pltpu.with_memory_space_constraint(arg, pltpu.HBM)
            for arg in (adjoint_in, forward_pops, solid_mask, region_label, design)
        )
    )


def solution(mesh):
    in_specs = (
        P(None, None, "gx", "gy"),
        P(None, None, None, "gx", "gy"),
        P(None, "gx", "gy"),
        P("gx", "gy"),
        P("gx", "gy"),
    )
    out_specs = (P(None, None, "gx", "gy"), P("gx", "gy"))
    return jax.shard_map(
        functools.partial(per_device, mesh.shape["gx"], mesh.shape["gy"]),
        mesh=mesh,
        in_specs=in_specs,
        out_specs=out_specs,
        check_vma=False,
    )
```

```python
import functools

import jax
import jax.numpy as jnp
from jax import lax
from jax.experimental import pallas as pl
from jax.experimental.pallas import tpu as pltpu
from jax.sharding import PartitionSpec as P

SWEEPS = 4
VELOCITIES = [
    (0, 0, 0),
    (1, 0, 0),
    (-1, 0, 0),
    (0, 1, 0),
    (0, -1, 0),
    (0, 0, 1),
    (0, 0, -1),
    (1, 1, 0),
    (-1, -1, 0),
    (1, -1, 0),
    (-1, 1, 0),
    (1, 0, 1),
    (-1, 0, -1),
    (1, 0, -1),
    (-1, 0, 1),
    (0, 1, 1),
    (0, -1, -1),
    (0, 1, -1),
    (0, -1, 1),
]
PAIRS = [VELOCITIES[2 * k + 1] for k in range(9)]
BLOCK_LIMIT = 0.5
SENSE_SCALE = 20.0
FILTER_WEIGHT = 16.0
MESH = pl.DeviceIdType.MESH
F32 = jnp.float32

DIRS = [(-1, 0), (1, 0), (0, -1), (0, 1), (-1, -1), (-1, 1), (1, -1), (1, 1)]


def pops_with(cx=None, cy=None):
    return [
        i
        for i, v in enumerate(VELOCITIES)
        if (cx is None or v[0] == cx) and (cy is None or v[1] == cy)
    ]


def add_all(terms):
    terms = list(terms)
    while len(terms) > 1:
        terms = [
            terms[k] + terms[k + 1] if k + 1 < len(terms) else terms[k]
            for k in range(0, len(terms), 2)
        ]
    return terms[0]


def along(values, axis):
    total = None
    for vel, val in zip(PAIRS, values):
        if vel[axis] == 0:
            continue
        if total is None:
            total = val if vel[axis] > 0 else -val
        else:
            total = total + val if vel[axis] > 0 else total - val
    return total


def dotted(vec, vel):
    total = None
    for comp, c in zip(vec, vel):
        if c == 0:
            continue
        if total is None:
            total = comp if c > 0 else -comp
        else:
            total = total + comp if c > 0 else total - comp
    return total


def adjoint_cell(f, a, blocking):
    fe = [f[2 * k + 1] + f[2 * k + 2] for k in range(9)]
    fo = [f[2 * k + 1] - f[2 * k + 2] for k in range(9)]
    rho = add_all([f[0]] + fe)
    inv = 1.0 / rho
    u = [along(fo, d) * inv for d in range(3)]
    usq = u[0] * u[0] + u[1] * u[1] + u[2] * u[2]

    e = [a[2 * k + 1] + a[2 * k + 2] for k in range(9)]
    o = [a[2 * k + 1] - a[2 * k + 2] for k in range(9)]
    mom = [0.28 * along(o, d) for d in range(3)]
    big_o = [1.4 * o[k] - dotted(mom, PAIRS[k]) for k in range(9)]
    edge = [e[3] + e[4], e[5] + e[6], e[7] + e[8]]
    axis_sum = e[0] + e[1] + e[2]
    edge_sum = edge[0] + edge[1] + edge[2]
    mean16 = (1.6 / 19.0) * (a[0] + axis_sum + edge_sum)
    a4 = 4.0 * a[0]
    t = [
        edge[0] - 2.0 * (e[0] + e[1]) + a4,
        edge[1] - 2.0 * (e[0] + e[2]) + a4,
        edge[2] - 2.0 * (e[1] + e[2]) + a4,
    ]
    tsum = (2.0 / 7.0) * (t[0] + t[1] + t[2])
    p = [(0.4 / 12.0) * (tk - tsum) for tk in t]
    b0 = 1.6 * a[0] - mean16 - 4.0 * (p[0] + p[1] + p[2])
    q = [-2.0 * (p[0] + p[1]), -2.0 * (p[0] + p[2]), -2.0 * (p[1] + p[2])]
    shift = [2.0 * (mean16 + val) for val in q + p]
    plane = [0, 1, 2, 3, 3, 4, 4, 5, 5]
    big_e = [1.6 * e[k] - shift[plane[k]] for k in range(9)]

    c36 = 1.0 / 36.0
    s3, s5, s7 = big_e[3] + big_e[4], big_e[5] + big_e[6], big_e[7] + big_e[8]
    zeroth = (1.0 / 3.0) * b0 + c36 * (
        2.0 * (big_e[0] + big_e[1] + big_e[2]) + s3 + s5 + s7
    )
    xx = c36 * (2.0 * big_e[0] + s3 + s5)
    yy = c36 * (2.0 * big_e[1] + s3 + s7)
    zz = c36 * (2.0 * big_e[2] + s5 + s7)
    xy = c36 * (big_e[3] - big_e[4])
    xz = c36 * (big_e[5] - big_e[6])
    yz = c36 * (big_e[7] - big_e[8])
    weighted = [2.0 * big_o[k] if k < 3 else big_o[k] for k in range(9)]
    first = [c36 * along(weighted, d) for d in range(3)]
    bu = [
        xx * u[0] + xy * u[1] + xz * u[2],
        xy * u[0] + yy * u[1] + yz * u[2],
        xz * u[0] + yz * u[1] + zz * u[2],
    ]
    ubu = 4.5 * (u[0] * bu[0] + u[1] * bu[1] + u[2] * bu[2])
    half_u = 1.5 * usq * zeroth
    scalar = zeroth + half_u - ubu
    vec = [3.0 * (first[d] - zeroth * u[d]) + 9.0 * bu[d] for d in range(3)]
    eq_b = zeroth - half_u + ubu + 3.0 * (
        first[0] * u[0] + first[1] * u[1] + first[2] * u[2]
    )

    open_part = 1.0 - blocking
    odd_keep = 1.0 - 2.0 * blocking
    result = [None] * 19
    result[0] = a[0] + open_part * (scalar - b0)
    half_open = 0.5 * open_part
    half_keep = 0.5 * odd_keep
    scalar2 = 2.0 * scalar
    vec2 = [2.0 * val for val in vec]
    for k in range(9):
        even = 0.5 * e[k] + half_open * (scalar2 - big_e[k])
        odd = half_keep * o[k] + half_open * (dotted(vec2, PAIRS[k]) - big_o[k])
        result[2 * k + 1] = even + odd
        result[2 * k + 2] = even - odd
    parts = [b0 * f[0] - rho * eq_b]
    for k in range(9):
        parts.append(0.5 * (big_e[k] * fe[k] + big_o[k] * fo[k]) - fo[k] * o[k])
    return result, add_all(parts)


def kernel(
    nx,
    ny,
    adj_hbm,
    pops_hbm,
    solid_hbm,
    label_hbm,
    design_hbm,
    out_ref,
    sens_ref,
    adj,
    pops,
    solid,
    label,
    design,
    mid,
    pull,
    send1,
    recv1,
    send2,
    recv2,
    send3,
    recv3,
    gath,
    part,
    in_sem,
    s_sem,
    r_sem,
    gs_sem,
    gr_sem,
):
    mx, my = lax.axis_index("gx"), lax.axis_index("gy")

    def has(d):
        conds = []
        if d[0] < 0:
            conds.append(mx > 0)
        if d[0] > 0:
            conds.append(mx < nx - 1)
        if d[1] < 0:
            conds.append(my > 0)
        if d[1] > 0:
            conds.append(my < ny - 1)
        return functools.reduce(jnp.logical_and, conds)

    barrier = pltpu.get_barrier_semaphore()
    count = nx * ny
    mine = mx * ny + my

    loads = [
        pltpu.make_async_copy(src, dst, in_sem.at[k])
        for k, (src, dst) in enumerate(
            [
                (label_hbm, label),
                (adj_hbm.at[pl.ds(0, 7)], adj.at[pl.ds(0, 7)]),
                (adj_hbm.at[pl.ds(7, 6)], adj.at[pl.ds(7, 6)]),
                (adj_hbm.at[pl.ds(13, 6)], adj.at[pl.ds(13, 6)]),
                (pops_hbm, pops),
                (solid_hbm, solid),
                (design_hbm, design),
            ]
        )
    ]
    for load in loads:
        load.start()

    def wrapped(pos, step, size):
        to = pos + step
        return jnp.where(to >= size, to - size, to)

    peer_x = [wrapped(mx, k, nx) for k in range(nx)]
    peer_y = [wrapped(my, k, ny) for k in range(ny)]

    def each_peer(body):
        if count <= 64:
            for k in range(1, count):
                body(k, (peer_x[k // ny], peer_y[k % ny]))
        else:

            @pl.loop(1, count)
            def _(k):
                body(k, (wrapped(mx, k // ny, nx), wrapped(my, lax.rem(k, ny), ny)))

    @each_peer
    def _(k, peer):
        pl.semaphore_signal(barrier, inc=1, device_id=peer, device_id_type=MESH)

    for n, d in enumerate(DIRS):

        @pl.when(jnp.logical_not(has((-d[0], -d[1]))))
        def _():
            for buf in (recv1, recv2, recv3):
                buf[n] = jnp.zeros(buf.shape[1:], F32)

    lane = lax.broadcasted_iota(jnp.int32, (16, 128), 1)
    lane4 = lax.broadcasted_iota(jnp.int32, (4, 128), 1)

    def copies(rnd, send, recv):
        out = []
        for n, d in enumerate(DIRS):
            rows = {0: (32, 16, 16), 1: (24, 16, 8), 2: (8, 16, 8)}[rnd][
                0 if d[1] == 0 else (1 if d[0] == 0 else 2)
            ]
            start = 0
            if rnd == 2 and d[0] > 0:
                start = 8
            src = send.at[pl.ds(start, rows)] if rnd == 2 else send.at[n, pl.ds(0, rows)]
            out.append(
                pltpu.make_async_remote_copy(
                    src_ref=src,
                    dst_ref=recv.at[n, pl.ds(0, rows)],
                    send_sem=s_sem.at[rnd, n],
                    recv_sem=r_sem.at[rnd, n],
                    device_id=(mx + d[0], my + d[1]),
                    device_id_type=MESH,
                )
            )
        return out

    def start_all(cps):
        for n, d in enumerate(DIRS):

            @pl.when(has(d))
            def _():
                cps[n].start()

    def recv_all(cps):
        for n, d in enumerate(DIRS):

            @pl.when(has((-d[0], -d[1])))
            def _():
                cps[n].wait_recv()

    def send_done(cps):
        for n, d in enumerate(DIRS):

            @pl.when(has(d))
            def _():
                cps[n].wait_send()

    def pack(src, send, region, cps=None):
        for n in (2, 3, 0, 1, 4, 5, 6, 7):
            dx, dy = DIRS[n]
            if dy == 0:
                row = 0 if dx < 0 else 15
                for j, i in enumerate(pops_with(cx=-dx)):
                    for z in range(4):
                        send[n, 4 * j + z : 4 * j + z + 1] = src[i, z, row : row + 1, :]
                if region is not None:
                    send[n, 24:32] = region[0:8] if dx < 0 else region[8:16]
            elif dx == 0:
                at = 0 if dy < 0 else 127
                base = 64 if dy < 0 else 0
                acc = region if region is not None else jnp.zeros((16, 128), F32)
                for j, i in enumerate(pops_with(cy=-dy)):
                    for z in range(4):
                        to = base + 4 * j + z
                        moved = pltpu.roll(src[i, z], (to - at) % 128, 1)
                        acc = jnp.where(lane == to, moved, acc)
                send[n, 0:16] = acc
            else:
                row = 0 if dx < 0 else 15
                i = VELOCITIES.index((-dx, -dy, 0))
                for z in range(4):
                    send[n, z : z + 1] = src[i, z, row : row + 1, :]
                if region is not None:
                    send[n, 8:16] = region[0:8] if dx < 0 else region[8:16]
            if cps is not None:

                @pl.when(has((dx, dy)))
                def _():
                    cps[n].start()

    def pull_local(src):
        for i, (cx, cy, cz) in enumerate(VELOCITIES):
            for z in range(4):
                val = src[i, z]
                if cy != 0:
                    val = pltpu.roll(val, (-cy) % 128, 1)
                pull[i, z, 8:24] = val

    def pull_edges(recv):
        for n, (dx, dy) in enumerate(DIRS):
            if dx == 0:
                base = 64 if dy < 0 else 0
                at = 127 if dy < 0 else 0
                got = recv[n, 0:16]
                for j, i in enumerate(pops_with(cy=-dy)):
                    for z in range(4):
                        moved = pltpu.roll(got, (at - base - 4 * j - z) % 128, 1)
                        pull[i, z, 8:24] = jnp.where(lane == at, moved, pull[i, z, 8:24])
            elif dy == 0:
                row = 24 if dx < 0 else 7
                for j, i in enumerate(pops_with(cx=-dx)):
                    cy = VELOCITIES[i][1]
                    val = recv[n, 4 * j : 4 * j + 4]
                    if cy != 0:
                        val = pltpu.roll(val, (-cy) % 128, 1)
                        corner = recv[DIRS.index((dx, -cy)), 0:4]
                        corner = pltpu.roll(corner, (-cy) % 128, 1)
                        val = jnp.where(lane4 == (127 if cy > 0 else 0), corner, val)
                    for z in range(4):
                        pull[i, z, row : row + 1] = val[z : z + 1]

    def cells(section, dst):
        total = None
        for z in range(4):
            f = [pops[section, i, z].astype(F32) for i in range(19)]
            a = []
            for i, (cx, cy, cz) in enumerate(VELOCITIES):
                a.append(pull[i, (z + cz) % 4, 8 + cx : 24 + cx, :])
            is_solid = solid[z] == 1
            inside = label[...] > 0
            blocking = jnp.where(
                is_solid, 1.0, jnp.where(inside, BLOCK_LIMIT * design[...], 0.0)
            )
            lever = jnp.where(
                jnp.logical_and(jnp.logical_not(is_solid), inside), BLOCK_LIMIT, 0.0
            )
            result, term = adjoint_cell(f, a, blocking)
            for i in range(19):
                dst[i, z] = result[i]
            term = term * lever
            total = term if total is None else total + term
        return total

    wide_row = lax.broadcasted_iota(jnp.int32, (32, 256), 0)
    wide_lane = lax.broadcasted_iota(jnp.int32, (32, 256), 1)
    gone = jnp.logical_or(
        jnp.logical_or(
            jnp.logical_and(wide_row >= 24, mx == 0),
            jnp.logical_and(
                jnp.logical_and(wide_row >= 16, wide_row < 24), mx == nx - 1
            ),
        ),
        jnp.logical_or(
            jnp.logical_and(wide_lane >= 192, my == 0),
            jnp.logical_and(
                jnp.logical_and(wide_lane >= 128, wide_lane < 192), my == ny - 1
            ),
        ),
    )
    scale_den = 1.0 / (1.0 + 4.0 * FILTER_WEIGHT)
    keep = jnp.where(gone, 0.0, scale_den)

    def widened(own, get):
        low = lane[0:8] < 64
        top = jnp.concatenate(
            [own, jnp.where(lane < 64, get((0, -1)), get((0, 1)))], axis=1
        )
        down = jnp.concatenate(
            [get((-1, 0)), jnp.where(low, get((-1, -1)), get((-1, 1)))], axis=1
        )
        up = jnp.concatenate(
            [get((1, 0)), jnp.where(low, get((1, -1)), get((1, 1)))], axis=1
        )
        return jnp.concatenate([top, down, up], axis=0)

    def jacobi(start):
        base = start * keep
        weight = FILTER_WEIGHT * keep
        smooth = jnp.where(gone, 0.0, start)
        for _ in range(SWEEPS):
            beside = (
                pltpu.roll(smooth, 1, 0)
                + pltpu.roll(smooth, 31, 0)
                + pltpu.roll(smooth, 1, 1)
                + pltpu.roll(smooth, 255, 1)
            )
            smooth = base + weight * beside
        return smooth

    for load in loads[:4]:
        load.wait()
    region = label[...].astype(F32)
    pack(adj, send1, region)
    pl.semaphore_wait(barrier, count - 1)
    cps1 = copies(0, send1, recv1)
    start_all(cps1)
    pull_local(adj)
    for load in loads[4:]:
        load.wait()
    recv_all(cps1)
    pull_edges(recv1)
    raw1 = cells(1, mid)

    cps2 = copies(1, send2, recv2)
    pack(mid, send2, None, cps2)
    pull_local(mid)

    def label_of(d):
        n = DIRS.index(d)
        if d[1] == 0:
            return recv1[n, 24:32]
        if d[0] == 0:
            return recv1[n, 0:16]
        return recv1[n, 8:16]

    wide_label = widened(region, label_of)
    share = []
    for r in (1.0, 2.0):
        share.append(jacobi(jnp.where(wide_label == r, 1.0, 0.0))[0:16, 0:128])

    quarter = lax.broadcasted_iota(jnp.int32, (1, 128), 1) // 32

    def folded(vals):
        row = jnp.zeros((1, 128), F32)
        for k, val in enumerate(vals):
            val = jnp.sum(val, axis=0, keepdims=True)
            val = val + pltpu.roll(val, 64, 1)
            val = val + pltpu.roll(val, 32, 1)
            row = jnp.where(quarter == k, val, row)
        return row

    zero = jnp.zeros((16, 128), F32)
    counts = folded(
        [zero, zero, jnp.where(region == 1.0, 1.0, 0.0), jnp.where(region == 2.0, 1.0, 0.0)]
    )

    recv_all(cps2)
    pull_edges(recv2)
    raw2 = cells(0, out_ref)
    raw = SENSE_SCALE * (raw1 + raw2)
    send3[...] = raw

    own_sums = folded([raw * share[0], raw * share[1]]) + counts
    part[...] = own_sums

    @each_peer
    def _(k, peer):
        pltpu.make_async_remote_copy(
            src_ref=part,
            dst_ref=gath.at[k - 1],
            send_sem=gs_sem.at[0],
            recv_sem=gr_sem.at[0],
            device_id=peer,
            device_id_type=MESH,
        ).start()

    cps3 = copies(2, send3, recv3)
    start_all(cps3)
    send_done(cps1)
    send_done(cps2)
    recv_all(cps3)

    def raw_of(d):
        n = DIRS.index(d)
        return recv3[n, 0:16] if d[0] == 0 else recv3[n, 0:8]

    smooth = jacobi(widened(raw, raw_of))[0:16, 0:128]

    send_done(cps3)
    pltpu.make_async_copy(gath, gath, gs_sem.at[0]).wait()
    pltpu.make_async_copy(gath, gath, gr_sem.at[0]).wait()
    total = own_sums + jnp.sum(gath[...], axis=0)
    tot = [
        jnp.sum(jnp.where(quarter == k, total, 0.0), axis=1, keepdims=True) for k in range(4)
    ]
    mean1 = tot[0] / jnp.maximum(tot[2], 1.0)
    mean2 = tot[1] / jnp.maximum(tot[3], 1.0)
    sens_ref[...] = jnp.where(
        region == 1.0, smooth - mean1, jnp.where(region == 2.0, smooth - mean2, 0.0)
    )


def per_device(nx, ny, adjoint_in, forward_pops, solid_mask, region_label, design):
    vmem, dma = pltpu.VMEM, pltpu.SemaphoreType.DMA
    return pl.pallas_call(
        functools.partial(kernel, nx, ny),
        out_shape=(
            jax.ShapeDtypeStruct(adjoint_in.shape, F32),
            jax.ShapeDtypeStruct(design.shape, F32),
        ),
        in_specs=[pl.BlockSpec(memory_space=pltpu.HBM)] * 5,
        out_specs=(
            pl.BlockSpec(memory_space=pltpu.VMEM),
            pl.BlockSpec(memory_space=pltpu.VMEM),
        ),
        scratch_shapes=[
            vmem(adjoint_in.shape, F32),
            vmem(forward_pops.shape, jnp.bfloat16),
            vmem(solid_mask.shape, jnp.int32),
            vmem(region_label.shape, jnp.int32),
            vmem(design.shape, F32),
            vmem(adjoint_in.shape, F32),
            vmem((19, 4, 32, 128), F32),
            vmem((8, 32, 128), F32),
            vmem((8, 32, 128), F32),
            vmem((8, 24, 128), F32),
            vmem((8, 24, 128), F32),
            vmem((16, 128), F32),
            vmem((8, 16, 128), F32),
            vmem((nx * ny - 1, 1, 128), F32),
            vmem((1, 128), F32),
            dma((7,)),
            dma((3, 8)),
            dma((3, 8)),
            dma((1,)),
            dma((1,)),
        ],
        compiler_params=pltpu.CompilerParams(
            collective_id=0, has_side_effects=True, vmem_limit_bytes=40 * 1024 * 1024
        ),
    )(
        *(
            pltpu.with_memory_space_constraint(arg, pltpu.HBM)
            for arg in (adjoint_in, forward_pops, solid_mask, region_label, design)
        )
    )


def solution(mesh):
    in_specs = (
        P(None, None, "gx", "gy"),
        P(None, None, None, "gx", "gy"),
        P(None, "gx", "gy"),
        P("gx", "gy"),
        P("gx", "gy"),
    )
    out_specs = (P(None, None, "gx", "gy"), P("gx", "gy"))
    return jax.shard_map(
        functools.partial(per_device, mesh.shape["gx"], mesh.shape["gy"]),
        mesh=mesh,
        in_specs=in_specs,
        out_specs=out_specs,
        check_vma=False,
    )
```
